32 devices in a mesh: lat: 4 (over z), lon: 8 (over y, x, core).
Axes of the slice: x: 2, y: 2, z: 4, core: 2. Of those that a mesh axis runs over, the one named last changes fastest.
Arguments:
- depth: float32 [512, 4096], P('lat', 'lon'), may hold values from 0 to 1
- soakage: float32 [512, 4096], P('lat', 'lon'), may hold values from 0.05 to 0.5
- elevation: float32 [512, 4096], P('lat', 'lon'), may hold values from -6 to 6
- roughness: float32 [512, 4096], P('lat', 'lon'), may hold values from 1 to 3
- conductivity: float32 [512, 4096], P('lat', 'lon'), may hold values from 0.05 to 1
- runoff: float32 [4, 32], P('lat', 'lon'), may hold values from 0.2 to 2
- coarse_index: int32 [512, 4096], P('lat', 'lon'), may hold values from 0 to 17, as said below
- wet_tiles: int32 [8, 64], P('lat', 'lon'), may hold values from 0 to 1, as said below
- channel_reach: int32 [512, 4096], P('lat', 'lon'), may hold values from 0 to 8192, as said below
- block_order: int32 [64], replicated, may hold values from 0 to 63, each once
Outputs:
- depth_out: float32 [512, 4096], P('lat', 'lon')
- soakage_out: float32 [512, 4096], P('lat', 'lon')
- reach_inflow: float32 [64, 128], P(('lat', 'lon'))
The draws below stay inside these ranges and needn't reach their ends.
Inputs may be any that keep to these rules, and one draw needn't show every extreme that they name: `coarse_index`: index into the device's runoff blocks with a rim of one block on each side, rows of 6 entries; the cell's block or one beside it. `wet_tiles`: 1 marks a wet tile. `channel_reach`: A reach index, or 8192 for a cell without a channel.
All inputs are finite; a program needn't handle non-finite values.
Results may differ from the reference program's by a relative error of at most 0.0001.
Values sent between devices are 32-bit elements; how exact they have to be, the bound alone decides.
A program may use at most 64 MiB of HBM per device.

```python
import math
import jax
import jax.numpy as jnp
from jax import lax

ROWS_DEV = 128
COLS_DEV = 512
COARSE = 128
TILE = 64
SUBSTEPS = 2
RB_DEV = 2
REACH_BLOCK = 128
NLAT = 512
NLON = 4096
NCLAT = 4
NCLON = 32
TLAT = 8
TLON = 64
BLOCKS = 64
REACHES = 8192


def draw_coarse_index(key, part):
    shape = (NLAT, NLON)
    row_ids = lax.broadcasted_iota(jnp.int32, shape, 0)
    col_ids = lax.broadcasted_iota(jnp.int32, shape, 1)
    local_row = row_ids % ROWS_DEV
    local_col = col_ids % COLS_DEV
    blocks_lon = COLS_DEV // COARSE
    margin = max(COARSE // 16, 1)
    first_key, second_key = jax.random.split(key)
    jitter_row = jax.random.randint(first_key, shape, -1, 2)
    jitter_col = jax.random.randint(second_key, shape, -1, 2)
    inner_row = local_row % COARSE
    inner_col = local_col % COARSE
    shift_row = jnp.where((inner_row < margin) & (jitter_row == -1), -1, jnp.where((inner_row >= COARSE - margin) & (jitter_row == 1), 1, 0))
    shift_col = jnp.where((inner_col < margin) & (jitter_col == -1), -1, jnp.where((inner_col >= COARSE - margin) & (jitter_col == 1), 1, 0))
    first_cell = (local_row == 0) & (local_col == 0)
    last_cell = (local_row == ROWS_DEV - 1) & (local_col == COLS_DEV - 1)
    shift_row = jnp.where(first_cell, -1, jnp.where(last_cell, 1, shift_row))
    shift_col = jnp.where(first_cell, -1, jnp.where(last_cell, 1, shift_col))
    block_row = local_row // COARSE + 1 + shift_row
    block_col = local_col // COARSE + 1 + shift_col
    return (block_row * (blocks_lon + 2) + block_col).astype(jnp.int32)


def draw_wet_tiles(key, part):
    shape = (TLAT, TLON)
    row_ids = lax.broadcasted_iota(jnp.int32, shape, 0)
    col_ids = lax.broadcasted_iota(jnp.int32, shape, 1)
    threshold = 15 + 70 * col_ids // TLON
    rolled = jax.random.randint(key, shape, 0, 100)
    wetness = jnp.where(rolled < threshold, 1, 0)
    wetness = jnp.where((row_ids == 0) & (col_ids == 0), 0, wetness)
    wetness = jnp.where((row_ids == TLAT - 1) & (col_ids == TLON - 1), 1, wetness)
    return wetness.astype(jnp.int32)


def draw_channel_reach(key, part):
    shape = (NLAT, NLON)
    row_ids = lax.broadcasted_iota(jnp.int32, shape, 0)
    col_ids = lax.broadcasted_iota(jnp.int32, shape, 1)
    lat_devices = NLAT // ROWS_DEV
    lon_devices = NLON // COLS_DEV
    first_key, second_key, third_key, fourth_key = jax.random.split(key, 4)
    is_channel = jax.random.randint(first_key, shape, 0, 8) == 0
    device_row = row_ids // ROWS_DEV
    device_col = col_ids // COLS_DEV
    target_kind = jax.random.randint(second_key, shape, 0, 4)
    target_row = jnp.where(target_kind == 1, (device_row + 1) % lat_devices, device_row)
    nearby = target_row * lon_devices + device_col
    anywhere = jax.random.randint(fourth_key, shape, 0, lat_devices * lon_devices)
    target = jnp.where(target_kind == 3, anywhere, nearby)
    reach_ids = target * (RB_DEV * REACH_BLOCK) + jax.random.randint(third_key, shape, 0, RB_DEV * REACH_BLOCK)
    result = jnp.where(is_channel, reach_ids, REACHES)
    result = jnp.where((row_ids == 0) & (col_ids == 0), REACHES, result)
    result = jnp.where((row_ids == 0) & (col_ids == 1), 0, result)
    return result.astype(jnp.int32)


def steps_of(rng, shape, shards, low, high):
    factor_of, own = 1.0, jax.random.fold_in(rng, 6)
    for position, blocks in shards:
        draws = jnp.exp(jax.random.uniform(jax.random.fold_in(own, position), (blocks,), jnp.float32, low / len(shards), high / len(shards)))
        factor_of = factor_of * jnp.repeat(draws, shape[position] // blocks).reshape([-1 if axis == position else 1 for axis in range(len(shape))])
    return factor_of


def scatter_about(stream_key, shape, scale, bound, pieces=(), held_as=jnp.bfloat16):
    level = steps_of(stream_key, shape, pieces, -0.22, 0.18) if pieces else 1.0
    entries = jax.random.normal(stream_key, shape, jnp.float32) * scale * level
    return jnp.minimum(jnp.maximum(entries, -bound), bound).astype(held_as)


def setup_inputs(seed: int = 0) -> dict:
    splits = jax.random.split(jax.random.key(seed), 11)
    return {
        "depth": jnp.clip(1.0 * jax.random.uniform(splits[0], (NLAT, NLON), jnp.float32) ** steps_of(splits[0], (NLAT, NLON), ((0, 4), (1, 8)), -0.2, 0.2), 0.0, 1.0),
        "soakage": jnp.clip(jnp.exp(math.log(0.5) - 2.3025851 * jax.random.uniform(splits[1], (NLAT, NLON), jnp.float32) ** steps_of(splits[1], (NLAT, NLON), ((0, 4), (1, 8)), -0.2, 0.2)), 0.05, 0.5),
        "elevation": scatter_about(splits[2], (NLAT, NLON), 0.5, 6.0, ((0, 4), (1, 8)), jnp.float32),
        "roughness": jnp.clip(jnp.exp(math.log(3.0) - 1.0986123 * jax.random.uniform(splits[3], (NLAT, NLON), jnp.float32) ** steps_of(splits[3], (NLAT, NLON), ((0, 4), (1, 8)), -0.2, 0.2)), 1.0, 3.0),
        "conductivity": jnp.clip(jnp.exp(math.log(1.0) - 2.9957323 * jax.random.uniform(splits[4], (NLAT, NLON), jnp.float32) ** steps_of(splits[4], (NLAT, NLON), ((0, 4), (1, 8)), -0.2, 0.2)), 0.05, 1.0),
        "runoff": jnp.clip(jnp.exp(math.log(2.0) - 2.3025851 * jax.random.uniform(splits[5], (NCLAT, NCLON), jnp.float32) ** steps_of(splits[5], (NCLAT, NCLON), ((0, 4), (1, 8)), -0.2, 0.2)), 0.2, 2.0),
        "coarse_index": draw_coarse_index(jax.random.fold_in(splits[10], 71), 0),
        "wet_tiles": draw_wet_tiles(jax.random.fold_in(splits[10], 71), 0),
        "channel_reach": draw_channel_reach(jax.random.fold_in(splits[10], 71), 0),
        "block_order": jax.random.permutation(splits[9], BLOCKS).astype(jnp.int32),
    }


time_step = 0.05
suction = 0.3
slope_floor = 0.25
drain_rate = 0.5

def power_five_thirds(value):
    return value * jnp.cbrt(value * value)

def face_flux(left_depth, right_depth, left_elev, right_elev, left_rough, right_rough, left_wet, right_wet):
    head_drop = left_elev + left_depth - (right_elev + right_depth)
    face_depth = 0.5 * (left_depth + right_depth)
    face_rough = 0.5 * (left_rough + right_rough)
    return left_wet * right_wet * power_five_thirds(face_depth) / face_rough * head_drop / jnp.sqrt(jnp.abs(head_drop) + slope_floor)

def outflow(depth_pad, elev_pad, rough_pad, wet_pad):
    eastward = face_flux(depth_pad[1:-1, :-1], depth_pad[1:-1, 1:], elev_pad[1:-1, :-1], elev_pad[1:-1, 1:], rough_pad[1:-1, :-1], rough_pad[1:-1, 1:], wet_pad[1:-1, :-1], wet_pad[1:-1, 1:])
    southward = face_flux(depth_pad[:-1, 1:-1], depth_pad[1:, 1:-1], elev_pad[:-1, 1:-1], elev_pad[1:, 1:-1], rough_pad[:-1, 1:-1], rough_pad[1:, 1:-1], wet_pad[:-1, 1:-1], wet_pad[1:, 1:-1])
    return eastward[:, 1:] - eastward[:, :-1] + southward[1:, :] - southward[:-1, :]

def reference(depth, soakage, elevation, roughness, conductivity, runoff, coarse_index, wet_tiles, channel_reach, block_order):
    nrows, ncols = depth.shape
    row_ids = lax.broadcasted_iota(jnp.int32, (nrows, ncols), 0)
    col_ids = lax.broadcasted_iota(jnp.int32, (nrows, ncols), 1)
    blocks_lat = ROWS_DEV // COARSE
    blocks_lon = COLS_DEV // COARSE
    rim_row = coarse_index // (blocks_lon + 2)
    rim_col = coarse_index % (blocks_lon + 2)
    coarse_row = (row_ids // ROWS_DEV * blocks_lat + rim_row).astype(jnp.int32)
    coarse_col = (col_ids // COLS_DEV * blocks_lon + rim_col).astype(jnp.int32)
    padded_runoff = jnp.pad(runoff, 1)
    cell_rate = padded_runoff[coarse_row, coarse_col]
    wet_cells = jnp.repeat(jnp.repeat(wet_tiles, TILE, 0), TILE, 1).astype(jnp.float32)
    channel = jnp.where(channel_reach < REACHES, wet_cells, jnp.float32(0.0))
    elev_pad = jnp.pad(elevation, 1)
    rough_pad = jnp.pad(roughness, 1)
    wet_pad = jnp.pad(wet_cells, 1)
    inflow_sum = jnp.zeros((REACHES + 1,), jnp.float32)
    level = depth
    soaked_sum = soakage
    for substep in range(SUBSTEPS):
        available = level + wet_cells * time_step * cell_rate
        potential = time_step * conductivity * (1.0 + suction / soaked_sum)
        soaked = wet_cells * jnp.minimum(potential, jnp.maximum(available, 0.0))
        ponded = available - soaked
        soaked_sum = soaked_sum + soaked
        routed = ponded - time_step * outflow(jnp.pad(ponded, 1), elev_pad, rough_pad, wet_pad)
        drained = channel * time_step * drain_rate * power_five_thirds(routed) / roughness
        level = routed - drained
        inflow_sum = inflow_sum + jax.ops.segment_sum(drained.reshape(-1), channel_reach.reshape(-1), num_segments=REACHES + 1)
    reach_inflow = inflow_sum[:REACHES].reshape(BLOCKS, REACH_BLOCK)[block_order]
    return (level, soaked_sum, reach_inflow)
```

```python
import functools
import math

import jax
import jax.numpy as jnp
from jax import lax
from jax.experimental import pallas as pl
from jax.experimental.pallas import tpu as pltpu
from jax.sharding import PartitionSpec as P

TILE = 64
REACH_BLOCK = 128
LANES = 128
BAND = 8
PACK = 16
MESH = pl.DeviceIdType.MESH

time_step = 0.05
suction = 0.3
slope_floor = 0.25
drain_rate = 0.5

FACE_SCALE = time_step * 2.0 * 0.5 ** (5.0 / 3.0)

STEPS = ((-1, 0), (1, 0), (0, -1), (0, 1), (-1, -1), (-1, 1), (1, -1), (1, 1))
OPPOSITE = (1, 0, 3, 2, 7, 6, 5, 4)
ELEV, ROUGH, WET, RATE = range(4)


def power_five_thirds(value):
    return value * jnp.exp2(jnp.log(value * value) * (1.0 / (3.0 * math.log(2.0))))


def face_flux(coef, depth_sum, head_drop):
    return (
        coef
        * power_five_thirds(depth_sum)
        * (head_drop * lax.rsqrt(jnp.abs(head_drop) + slope_floor))
    )


def infiltrate(level, soaked_sum, conductivity, supply, wet):
    available = level + supply
    potential = time_step * conductivity * (1.0 + suction / soaked_sum)
    soaked = wet * jnp.minimum(potential, jnp.maximum(available, 0.0))
    return available - soaked, soaked_sum + soaked


def kernel(
    n_lat,
    n_lon,
    depth,
    soakage,
    elevation,
    roughness,
    conductivity,
    runoff,
    coarse,
    wet_tiles,
    reach,
    order,
    depth_out,
    soak_out,
    inflow_out,
    wet_rows,
    ponded,
    resid,
    supply,
    coef_e,
    coef_s,
    coef_d,
    drained_sum,
    own_edge,
    near_edge,
    near_corner,
    own_depth,
    near_depth,
    totals,
    arrived,
    edge_send,
    edge_recv,
    depth_send,
    depth_recv,
    total_send,
    total_recv,
):
    rows, cols = depth.shape
    bands = rows // BAND
    chunks = cols // LANES
    blocks = order.shape[0]
    n_dev = n_lat * n_lon
    per_dev = blocks // n_dev
    num_reaches = blocks * REACH_BLOCK
    lat, lon = lax.axis_index("lat"), lax.axis_index("lon")
    me = lat * n_lon + lon

    near_edge[...] = jnp.zeros_like(near_edge)
    near_corner[...] = jnp.zeros_like(near_corner)
    near_depth[...] = jnp.zeros_like(near_depth)

    barrier = pltpu.get_barrier_semaphore()

    def other(offset):
        device = lax.rem(me + offset, n_dev)
        return (lax.div(device, n_lon), lax.rem(device, n_lon))

    @pl.loop(1, n_dev)
    def _(offset):
        pl.semaphore_signal(barrier, inc=1, device_id=other(offset), device_id_type=MESH)

    def on_side(side, action):
        up, right = STEPS[side]
        row, col = lat + up, lon + right
        inside = (row >= 0) & (row < n_lat) & (col >= 0) & (col < n_lon)

        @pl.when(inside)
        def _():
            action((row, col))

    def edge_copy(side, device, slot):
        if side < 4:
            src, dst = own_edge.at[side], near_edge.at[slot]
        else:
            src, dst = own_edge.at[0, RATE], near_corner.at[slot - 4]
        return pltpu.make_async_remote_copy(
            src_ref=src,
            dst_ref=dst,
            send_sem=edge_send.at[side],
            recv_sem=edge_recv.at[slot],
            device_id=device,
            device_id_type=MESH,
        )

    def depth_copy(step, side, device, slot):
        return pltpu.make_async_remote_copy(
            src_ref=own_depth.at[step, side],
            dst_ref=near_depth.at[step, slot],
            send_sem=depth_send.at[step, side],
            recv_sem=depth_recv.at[step, slot],
            device_id=device,
            device_id_type=MESH,
        )

    def total_copy(offset):
        device = lax.rem(me + offset, n_dev)
        return pltpu.make_async_remote_copy(
            src_ref=totals.at[device],
            dst_ref=arrived.at[offset],
            send_sem=total_send.at[offset],
            recv_sem=total_recv.at[offset],
            device_id=(lax.div(device, n_lon), lax.rem(device, n_lon)),
            device_id_type=MESH,
        )

    lane = lax.broadcasted_iota(jnp.int32, (BAND, LANES), 1)
    wide_lane = lax.broadcasted_iota(jnp.int32, (BAND, cols), 1)
    wide_row = lax.broadcasted_iota(jnp.int32, (BAND, cols), 0)
    square_row = lax.broadcasted_iota(jnp.int32, (rows, LANES), 0)
    square_lane = lax.broadcasted_iota(jnp.int32, (rows, LANES), 1)
    diagonal = square_row == square_lane

    def band_at(ref, b):
        return ref[pl.ds(pl.multiple_of(b * BAND, BAND), BAND), :]

    def put_band(ref, b, value):
        ref[pl.ds(pl.multiple_of(b * BAND, BAND), BAND), :] = value

    def wet_at(b):
        return band_at(wet_rows, lax.div(b, TILE // BAND))

    def below(here, after):
        return pltpu.roll(jnp.where(wide_row == 0, after, here), BAND - 1, 0)

    def above(before, here):
        return pltpu.roll(jnp.where(wide_row == BAND - 1, before, here), 1, 0)

    def east(here):
        return pltpu.roll(here, cols - 1, 1)

    def west(here):
        return pltpu.roll(here, 1, 1)

    def as_row(column):
        return jnp.sum(jnp.where(diagonal, column, 0.0), axis=0, keepdims=True)

    def as_column(row):
        return jnp.sum(jnp.where(diagonal, row, 0.0), axis=1, keepdims=True)

    def pack_edges(ref, put):
        for c in range(chunks):
            cut = slice(c * LANES, (c + 1) * LANES)
            put(0, c, ref[0:1, cut])
            put(1, c, ref[rows - 1 : rows, cut])
        put(2, 0, as_row(ref[:, 0:LANES][:, 0:1]))
        put(3, 0, as_row(ref[:, cols - LANES : cols][:, LANES - 1 : LANES]))

    tile_rows, tile_cols = wet_tiles.shape
    for tr in range(tile_rows):
        value = jnp.zeros((BAND, cols), jnp.float32)
        for tc in range(tile_cols):
            inside = (wide_lane >= tc * TILE) & (wide_lane < (tc + 1) * TILE)
            value = jnp.where(inside, wet_tiles[tr, tc].astype(jnp.float32), value)
        wet_rows[tr * BAND : (tr + 1) * BAND, :] = value

    own_edge[...] = jnp.zeros_like(own_edge)
    own_depth[...] = jnp.zeros_like(own_depth)

    def put_field(field):
        def put(side, line, value):
            own_edge[side, field, line : line + 1, :] = value

        return put

    pack_edges(elevation, put_field(ELEV))
    pack_edges(roughness, put_field(ROUGH))
    last_tile = (tile_rows - 1) * BAND
    for c in range(chunks):
        cut = slice(c * LANES, (c + 1) * LANES)
        own_edge[0, WET, c : c + 1, :] = wet_rows[0:1, cut]
        own_edge[1, WET, c : c + 1, :] = wet_rows[last_tile : last_tile + 1, cut]
    row_lane = lax.broadcasted_iota(jnp.int32, (1, LANES), 1)
    for side, tc in ((2, 0), (3, tile_cols - 1)):
        value = jnp.zeros((1, LANES), jnp.float32)
        for tr in range(tile_rows):
            inside = (row_lane >= tr * TILE) & (row_lane < (tr + 1) * TILE)
            value = jnp.where(inside, wet_tiles[tr, tc].astype(jnp.float32), value)
        own_edge[side, WET, 0:1, :] = value
    block_cols = runoff.shape[1]
    rates = jnp.zeros((BAND, LANES), jnp.float32)
    for c in range(block_cols):
        rates = jnp.where(lane == c, runoff[0, c], rates)
    for side in range(4):
        own_edge[side, RATE] = rates

    pl.semaphore_wait(barrier, n_dev - 1)
    for side in range(8):
        on_side(side, lambda device, side=side: edge_copy(side, device, OPPOSITE[side]).start())

    @pl.loop(0, bands)
    def _(b):
        after = jnp.minimum(b + 1, bands - 1)
        rough, wet = band_at(roughness, b), wet_at(b)
        rough_s = below(rough, band_at(roughness, after))
        wet_s = below(wet, wet_at(after))
        value = FACE_SCALE * wet * wet_s / (rough + rough_s)
        put_band(coef_s, b, jnp.where(wide_row + b * BAND == rows - 1, 0.0, value))
        value = FACE_SCALE * wet * east(wet) / (rough + east(rough))
        put_band(coef_e, b, jnp.where(wide_lane == cols - 1, 0.0, value))
        channel = jnp.where(band_at(reach, b) < num_reaches, wet, 0.0)
        put_band(coef_d, b, channel * (time_step * drain_rate) / rough)

    for side in range(8):
        on_side(side, lambda device, side=side: edge_copy(side, device, side).wait_recv())

    def entry(ref_tile, c):
        return jnp.broadcast_to(ref_tile[0:1, c : c + 1], (BAND, cols))

    def rate_row(left, middle, right):
        return (
            [entry(left, block_cols - 1)]
            + [entry(middle, c) for c in range(block_cols)]
            + [entry(right, 0)]
        )

    table = (
        rate_row(near_corner[0], near_edge[0, RATE], near_corner[1])
        + rate_row(near_edge[2, RATE], rates, near_edge[3, RATE])
        + rate_row(near_corner[2], near_edge[1, RATE], near_corner[3])
    )

    @pl.loop(0, bands)
    def _(b):
        index = band_at(coarse, b)
        wet = wet_at(b)
        rate = table[0]
        for k in range(1, len(table)):
            rate = jnp.where(index == k, table[k], rate)
        water = wet * time_step * rate
        put_band(supply, b, water)
        h, soaked = infiltrate(
            band_at(depth, b), band_at(soakage, b), band_at(conductivity, b), water, wet
        )
        put_band(ponded, b, h)
        put_band(soak_out, b, soaked)

    edge_rough = jnp.maximum(own_edge[:, ROUGH] + near_edge[:, ROUGH], 1.0)
    edge_coef = FACE_SCALE * own_edge[:, WET] * near_edge[:, WET] / edge_rough
    edge_drop = own_edge[:, ELEV] - near_edge[:, ELEV]

    def send_depth(step):
        def put(side, line, value):
            own_depth[step, side, line : line + 1, :] = value

        pack_edges(ponded, put)
        for side in range(4):
            on_side(
                side,
                lambda device, side=side: depth_copy(step, side, device, OPPOSITE[side]).start(),
            )

    def route(step):
        def body(b, flux_n):
            after = jnp.minimum(b + 1, bands - 1)
            h, h_after = band_at(ponded, b), band_at(ponded, after)
            head = band_at(elevation, b) + h
            head_after = band_at(elevation, after) + h_after
            flux_s = face_flux(
                band_at(coef_s, b), h + below(h, h_after), head - below(head, head_after)
            )
            flux_e = face_flux(band_at(coef_e, b), h + east(h), head - east(head))
            out = flux_e - west(flux_e) + flux_s - above(flux_n, flux_s)
            put_band(resid, b, h - out)
            return flux_s

        lax.fori_loop(0, bands, body, jnp.zeros((BAND, cols), jnp.float32))
        for side in range(4):
            on_side(
                side, lambda device, side=side: depth_copy(step, side, device, side).wait_recv()
            )
        mine, theirs = own_depth[step], near_depth[step]
        out = face_flux(edge_coef, mine + theirs, edge_drop + (mine - theirs))
        for c in range(chunks):
            cut = slice(c * LANES, (c + 1) * LANES)
            resid[0:1, cut] = resid[0:1, cut] - out[0, c : c + 1, :]
            resid[rows - 1 : rows, cut] = resid[rows - 1 : rows, cut] - out[1, c : c + 1, :]
        first, last = slice(0, LANES), slice(cols - LANES, cols)
        column = as_column(out[2, 0:1, :])
        resid[:, first] = resid[:, first] - jnp.where(square_lane == 0, column, 0.0)
        column = as_column(out[3, 0:1, :])
        resid[:, last] = resid[:, last] - jnp.where(square_lane == LANES - 1, column, 0.0)

    send_depth(0)
    route(0)

    @pl.loop(0, bands)
    def _(b):
        routed = band_at(resid, b)
        drained = band_at(coef_d, b) * power_five_thirds(routed)
        put_band(drained_sum, b, drained)
        h, soaked = infiltrate(
            routed - drained,
            band_at(soak_out, b),
            band_at(conductivity, b),
            band_at(supply, b),
            wet_at(b),
        )
        put_band(ponded, b, h)
        put_band(soak_out, b, soaked)

    send_depth(1)
    route(1)

    pack_row = lax.broadcasted_iota(jnp.int32, (PACK, LANES), 0)
    lines = [
        (pack_row + t * PACK).astype(jnp.float32).astype(jnp.bfloat16)
        for t in range(REACH_BLOCK // PACK)
    ]
    owners = []
    for t in range(blocks // PACK):
        value = jnp.zeros((PACK, LANES), jnp.int32)
        for i in range(PACK):
            value = jnp.where(pack_row == i, order[t * PACK + i], value)
        owners.append(value.astype(jnp.float32).astype(jnp.bfloat16))
    one = jnp.ones((PACK, LANES), jnp.bfloat16)
    zero = jnp.zeros((PACK, LANES), jnp.bfloat16)

    def drain(b, total):
        routed = band_at(resid, b)
        drained = band_at(coef_d, b) * power_five_thirds(routed)
        put_band(depth_out, b, routed - drained)
        value = band_at(drained_sum, b) + drained
        upper = value.astype(jnp.bfloat16).astype(jnp.float32)
        lower = value - upper
        cell = band_at(reach, b)
        block = lax.shift_right_logical(cell, 7).astype(jnp.float32)
        line = lax.bitwise_and(cell, REACH_BLOCK - 1).astype(jnp.float32)
        for i in range(BAND):

            def spread(x, c):
                row = x[i : i + 1, c * LANES : (c + 1) * LANES]
                return jnp.broadcast_to(row, (PACK, LANES)).astype(jnp.bfloat16)

            left, right = [], []
            for c in range(chunks):
                block_c, line_c = spread(block, c), spread(line, c)
                upper_c, lower_c = spread(upper, c), spread(lower, c)
                hits = [block_c == o for o in owners]
                left.append(
                    jnp.concatenate(
                        [jnp.where(hit, upper_c, zero) for hit in hits]
                        + [jnp.where(hit, lower_c, zero) for hit in hits],
                        axis=0,
                    )
                )
                right.append(
                    jnp.concatenate([jnp.where(line_c == o, one, zero) for o in lines], axis=0)
                )
            total = total + lax.dot_general(
                jnp.concatenate(left, axis=1),
                jnp.concatenate(right, axis=1),
                (((1,), (1,)), ((), ())),
                preferred_element_type=jnp.float32,
            )
        return total

    total = lax.fori_loop(
        0, bands, drain, jnp.zeros((2 * blocks, REACH_BLOCK), jnp.float32)
    )
    total = total[:blocks] + total[blocks:]
    for d in range(n_dev):
        totals[d] = total[d * per_dev : (d + 1) * per_dev]

    @pl.loop(1, n_dev)
    def _(offset):
        total_copy(offset).start()

    arrived[0] = totals[me]

    for side in range(8):
        on_side(side, lambda device, side=side: edge_copy(side, device, side).wait_send())
    for step in range(2):
        for side in range(4):
            on_side(
                side,
                lambda device, side=side, step=step: depth_copy(
                    step, side, device, side
                ).wait_send(),
            )

    @pl.loop(1, n_dev)
    def _(offset):
        total_copy(offset).wait_recv()

    inflow_out[...] = jnp.sum(arrived[...], axis=0)

    @pl.loop(1, n_dev)
    def _(offset):
        total_copy(offset).wait_send()


def shards(n_lat, n_lon, *operands):
    depth, order = operands[0], operands[9]
    rows, cols = depth.shape
    tile_rows = operands[7].shape[0]
    n_dev = n_lat * n_lon
    per_dev = order.shape[0] // n_dev
    vmem, smem = pl.BlockSpec(memory_space=pltpu.VMEM), pl.BlockSpec(memory_space=pltpu.SMEM)
    grid = pltpu.VMEM((rows, cols), jnp.float32)
    return pl.pallas_call(
        functools.partial(kernel, n_lat, n_lon),
        out_shape=(
            jax.ShapeDtypeStruct((rows, cols), jnp.float32),
            jax.ShapeDtypeStruct((rows, cols), jnp.float32),
            jax.ShapeDtypeStruct((per_dev, REACH_BLOCK), jnp.float32),
        ),
        in_specs=[vmem] * 5 + [smem, vmem, smem, vmem, smem],
        out_specs=(vmem, vmem, vmem),
        scratch_shapes=[
            pltpu.VMEM((tile_rows * BAND, cols), jnp.float32),
            grid,
            grid,
            grid,
            grid,
            grid,
            grid,
            grid,
            pltpu.VMEM((4, 4, BAND, LANES), jnp.float32),
            pltpu.VMEM((4, 4, BAND, LANES), jnp.float32),
            pltpu.VMEM((4, BAND, LANES), jnp.float32),
            pltpu.VMEM((2, 4, BAND, LANES), jnp.float32),
            pltpu.VMEM((2, 4, BAND, LANES), jnp.float32),
            pltpu.VMEM((n_dev, per_dev, REACH_BLOCK), jnp.float32),
            pltpu.VMEM((n_dev, per_dev, REACH_BLOCK), jnp.float32),
            pltpu.SemaphoreType.DMA((8,)),
            pltpu.SemaphoreType.DMA((8,)),
            pltpu.SemaphoreType.DMA((2, 4)),
            pltpu.SemaphoreType.DMA((2, 4)),
            pltpu.SemaphoreType.DMA((n_dev,)),
            pltpu.SemaphoreType.DMA((n_dev,)),
        ],
        compiler_params=pltpu.CompilerParams(
            collective_id=0, has_side_effects=True, vmem_limit_bytes=40 * 1024 * 1024
        ),
        name="flow",
    )(*operands)


def solution(mesh):
    placed = (P("lat", "lon"),) * 9 + (P(),)
    return jax.shard_map(
        functools.partial(shards, mesh.shape["lat"], mesh.shape["lon"]),
        mesh=mesh,
        in_specs=placed,
        out_specs=(P("lat", "lon"), P("lat", "lon"), P(("lat", "lon"), None)),
        check_vma=False,
    )
```

```python
import functools
import math

import jax
import jax.numpy as jnp
from jax import lax
from jax.experimental import pallas as pl
from jax.experimental.pallas import tpu as pltpu
from jax.sharding import PartitionSpec as P

TILE = 64
REACH_BLOCK = 128
LANES = 128
BAND = 8
PACK = 16
VMEM_LIMIT = 60 * 1024 * 1024
MESH = pl.DeviceIdType.MESH

time_step = 0.05
suction = 0.3
slope_floor = 0.25
drain_rate = 0.5

FACE_SCALE = time_step * 2.0 * 0.5 ** (5.0 / 3.0)

STEPS = ((-1, 0), (1, 0), (0, -1), (0, 1), (-1, -1), (-1, 1), (1, -1), (1, 1))
OPPOSITE = (1, 0, 3, 2, 7, 6, 5, 4)
ELEV, ROUGH, WET, RATE = range(4)


def power_five_thirds(value):
    return value * jnp.exp2(jnp.log(value * value) * (1.0 / (3.0 * math.log(2.0))))


def face_flux(coef, depth_sum, head_drop):
    return (
        coef
        * power_five_thirds(depth_sum)
        * (head_drop * lax.rsqrt(jnp.abs(head_drop) + slope_floor))
    )


def infiltrate(level, soaked_sum, conductivity, supply, wet):
    available = level + supply
    potential = time_step * conductivity * (1.0 + suction / soaked_sum)
    soaked = wet * jnp.minimum(potential, jnp.maximum(available, 0.0))
    return available - soaked, soaked_sum + soaked


def kernel(
    n_lat,
    n_lon,
    depth_hbm,
    soakage_hbm,
    elevation_hbm,
    roughness_hbm,
    conductivity_hbm,
    runoff_hbm,
    coarse_hbm,
    wet_tiles_hbm,
    reach_hbm,
    order_hbm,
    depth_out_hbm,
    soak_out_hbm,
    inflow_out_hbm,
    depth,
    soakage,
    elevation,
    roughness,
    conductivity,
    runoff,
    coarse,
    wet_tiles,
    reach,
    order,
    depth_out,
    soak_out,
    inflow_out,
    load_sem,
    save_sem,
    wet_rows,
    ponded,
    resid,
    supply,
    coef_e,
    coef_s,
    coef_d,
    drained_sum,
    own_edge,
    near_edge,
    near_corner,
    own_depth,
    near_depth,
    totals,
    arrived,
    edge_send,
    edge_recv,
    depth_send,
    depth_recv,
    total_send,
    total_recv,
):
    rows, cols = depth.shape
    bands = rows // BAND
    chunks = cols // LANES
    blocks = order.shape[0]
    n_dev = n_lat * n_lon
    per_dev = blocks // n_dev
    num_reaches = blocks * REACH_BLOCK
    lat, lon = lax.axis_index("lat"), lax.axis_index("lon")
    me = lat * n_lon + lon

    loads = [
        pltpu.make_async_copy(src, dst, load_sem.at[k])
        for k, (src, dst) in enumerate(
            (
                (wet_tiles_hbm, wet_tiles),
                (runoff_hbm, runoff),
                (elevation_hbm, elevation),
                (roughness_hbm, roughness),
                (reach_hbm, reach),
                (order_hbm, order),
                (coarse_hbm, coarse),
                (depth_hbm, depth),
                (soakage_hbm, soakage),
                (conductivity_hbm, conductivity),
            )
        )
    ]
    for load in loads:
        load.start()
    near_edge[...] = jnp.zeros_like(near_edge)
    near_corner[...] = jnp.zeros_like(near_corner)
    near_depth[...] = jnp.zeros_like(near_depth)

    barrier = pltpu.get_barrier_semaphore()

    def other(offset):
        device = lax.rem(me + offset, n_dev)
        return (lax.div(device, n_lon), lax.rem(device, n_lon))

    @pl.loop(1, n_dev)
    def _(offset):
        pl.semaphore_signal(barrier, inc=1, device_id=other(offset), device_id_type=MESH)

    def on_side(side, action):
        up, right = STEPS[side]
        row, col = lat + up, lon + right
        inside = (row >= 0) & (row < n_lat) & (col >= 0) & (col < n_lon)

        @pl.when(inside)
        def _():
            action((row, col))

    def edge_copy(side, device, slot):
        if side < 4:
            src, dst = own_edge.at[side], near_edge.at[slot]
        else:
            src, dst = own_edge.at[0, RATE], near_corner.at[slot - 4]
        return pltpu.make_async_remote_copy(
            src_ref=src,
            dst_ref=dst,
            send_sem=edge_send.at[side],
            recv_sem=edge_recv.at[slot],
            device_id=device,
            device_id_type=MESH,
        )

    def depth_copy(step, side, device, slot):
        return pltpu.make_async_remote_copy(
            src_ref=own_depth.at[step, side],
            dst_ref=near_depth.at[step, slot],
            send_sem=depth_send.at[step, side],
            recv_sem=depth_recv.at[step, slot],
            device_id=device,
            device_id_type=MESH,
        )

    def total_copy(offset):
        device = lax.rem(me + offset, n_dev)
        return pltpu.make_async_remote_copy(
            src_ref=totals.at[device],
            dst_ref=arrived.at[offset],
            send_sem=total_send.at[offset],
            recv_sem=total_recv.at[offset],
            device_id=(lax.div(device, n_lon), lax.rem(device, n_lon)),
            device_id_type=MESH,
        )

    lane = lax.broadcasted_iota(jnp.int32, (BAND, LANES), 1)
    wide_lane = lax.broadcasted_iota(jnp.int32, (BAND, cols), 1)
    wide_row = lax.broadcasted_iota(jnp.int32, (BAND, cols), 0)
    square_row = lax.broadcasted_iota(jnp.int32, (rows, LANES), 0)
    square_lane = lax.broadcasted_iota(jnp.int32, (rows, LANES), 1)
    diagonal = square_row == square_lane

    def band_at(ref, b):
        return ref[pl.ds(pl.multiple_of(b * BAND, BAND), BAND), :]

    def put_band(ref, b, value):
        ref[pl.ds(pl.multiple_of(b * BAND, BAND), BAND), :] = value

    def wet_at(b):
        return band_at(wet_rows, lax.div(b, TILE // BAND))

    def below(here, after):
        return pltpu.roll(jnp.where(wide_row == 0, after, here), BAND - 1, 0)

    def above(before, here):
        return pltpu.roll(jnp.where(wide_row == BAND - 1, before, here), 1, 0)

    def east(here):
        return pltpu.roll(here, cols - 1, 1)

    def west(here):
        return pltpu.roll(here, 1, 1)

    def as_row(column):
        return jnp.sum(jnp.where(diagonal, column, 0.0), axis=0, keepdims=True)

    def as_column(row):
        return jnp.sum(jnp.where(diagonal, row, 0.0), axis=1, keepdims=True)

    def pack_edges(ref, put):
        for c in range(chunks):
            cut = slice(c * LANES, (c + 1) * LANES)
            put(0, c, ref[0:1, cut])
            put(1, c, ref[rows - 1 : rows, cut])
        put(2, 0, as_row(ref[:, 0:LANES][:, 0:1]))
        put(3, 0, as_row(ref[:, cols - LANES : cols][:, LANES - 1 : LANES]))

    for load in loads[:4]:
        load.wait()

    tile_rows, tile_cols = wet_tiles.shape
    for tr in range(tile_rows):
        value = jnp.zeros((BAND, cols), jnp.float32)
        for tc in range(tile_cols):
            inside = (wide_lane >= tc * TILE) & (wide_lane < (tc + 1) * TILE)
            value = jnp.where(inside, wet_tiles[tr, tc].astype(jnp.float32), value)
        wet_rows[tr * BAND : (tr + 1) * BAND, :] = value

    own_edge[...] = jnp.zeros_like(own_edge)
    own_depth[...] = jnp.zeros_like(own_depth)

    def put_field(field):
        def put(side, line, value):
            own_edge[side, field, line : line + 1, :] = value

        return put

    pack_edges(elevation, put_field(ELEV))
    pack_edges(roughness, put_field(ROUGH))
    last_tile = (tile_rows - 1) * BAND
    for c in range(chunks):
        cut = slice(c * LANES, (c + 1) * LANES)
        own_edge[0, WET, c : c + 1, :] = wet_rows[0:1, cut]
        own_edge[1, WET, c : c + 1, :] = wet_rows[last_tile : last_tile + 1, cut]
    row_lane = lax.broadcasted_iota(jnp.int32, (1, LANES), 1)
    for side, tc in ((2, 0), (3, tile_cols - 1)):
        value = jnp.zeros((1, LANES), jnp.float32)
        for tr in range(tile_rows):
            inside = (row_lane >= tr * TILE) & (row_lane < (tr + 1) * TILE)
            value = jnp.where(inside, wet_tiles[tr, tc].astype(jnp.float32), value)
        own_edge[side, WET, 0:1, :] = value
    block_cols = runoff.shape[1]
    rates = jnp.zeros((BAND, LANES), jnp.float32)
    for c in range(block_cols):
        rates = jnp.where(lane == c, runoff[0, c], rates)
    for side in range(4):
        own_edge[side, RATE] = rates

    pl.semaphore_wait(barrier, n_dev - 1)
    for side in range(8):
        on_side(side, lambda device, side=side: edge_copy(side, device, OPPOSITE[side]).start())

    for load in loads[4:]:
        load.wait()

    @pl.loop(0, bands, unroll=2)
    def _(b):
        after = jnp.minimum(b + 1, bands - 1)
        rough, wet = band_at(roughness, b), wet_at(b)
        rough_s = below(rough, band_at(roughness, after))
        wet_s = below(wet, wet_at(after))
        value = FACE_SCALE * wet * wet_s / (rough + rough_s)
        put_band(coef_s, b, jnp.where(wide_row + b * BAND == rows - 1, 0.0, value))
        value = FACE_SCALE * wet * east(wet) / (rough + east(rough))
        put_band(coef_e, b, jnp.where(wide_lane == cols - 1, 0.0, value))
        channel = jnp.where(band_at(reach, b) < num_reaches, wet, 0.0)
        put_band(coef_d, b, channel * (time_step * drain_rate) / rough)

    for side in range(8):
        on_side(side, lambda device, side=side: edge_copy(side, device, side).wait_recv())

    def entry(ref_tile, c):
        return jnp.broadcast_to(ref_tile[0:1, c : c + 1], (BAND, cols))

    def rate_row(left, middle, right):
        return (
            [entry(left, block_cols - 1)]
            + [entry(middle, c) for c in range(block_cols)]
            + [entry(right, 0)]
        )

    table = (
        rate_row(near_corner[0], near_edge[0, RATE], near_corner[1])
        + rate_row(near_edge[2, RATE], rates, near_edge[3, RATE])
        + rate_row(near_corner[2], near_edge[1, RATE], near_corner[3])
    )

    @pl.loop(0, bands, unroll=2)
    def _(b):
        index = band_at(coarse, b)
        wet = wet_at(b)
        rate = table[0]
        for k in range(1, len(table)):
            rate = jnp.where(index == k, table[k], rate)
        water = wet * time_step * rate
        put_band(supply, b, water)
        h, soaked = infiltrate(
            band_at(depth, b), band_at(soakage, b), band_at(conductivity, b), water, wet
        )
        put_band(ponded, b, h)
        put_band(soak_out, b, soaked)

    edge_rough = jnp.maximum(own_edge[:, ROUGH] + near_edge[:, ROUGH], 1.0)
    edge_coef = FACE_SCALE * own_edge[:, WET] * near_edge[:, WET] / edge_rough
    edge_drop = own_edge[:, ELEV] - near_edge[:, ELEV]

    def send_depth(step):
        def put(side, line, value):
            own_depth[step, side, line : line + 1, :] = value

        pack_edges(ponded, put)
        for side in range(4):
            on_side(
                side,
                lambda device, side=side: depth_copy(step, side, device, OPPOSITE[side]).start(),
            )

    def route(step):
        def body(b, flux_n):
            after = jnp.minimum(b + 1, bands - 1)
            h, h_after = band_at(ponded, b), band_at(ponded, after)
            head = band_at(elevation, b) + h
            head_after = band_at(elevation, after) + h_after
            flux_s = face_flux(
                band_at(coef_s, b), h + below(h, h_after), head - below(head, head_after)
            )
            flux_e = face_flux(band_at(coef_e, b), h + east(h), head - east(head))
            out = flux_e - west(flux_e) + flux_s - above(flux_n, flux_s)
            put_band(resid, b, h - out)
            return flux_s

        lax.fori_loop(0, bands, body, jnp.zeros((BAND, cols), jnp.float32), unroll=2)
        for side in range(4):
            on_side(
                side, lambda device, side=side: depth_copy(step, side, device, side).wait_recv()
            )
        mine, theirs = own_depth[step], near_depth[step]
        out = face_flux(edge_coef, mine + theirs, edge_drop + (mine - theirs))
        for c in range(chunks):
            cut = slice(c * LANES, (c + 1) * LANES)
            resid[0:1, cut] = resid[0:1, cut] - out[0, c : c + 1, :]
            resid[rows - 1 : rows, cut] = resid[rows - 1 : rows, cut] - out[1, c : c + 1, :]
        first, last = slice(0, LANES), slice(cols - LANES, cols)
        column = as_column(out[2, 0:1, :])
        resid[:, first] = resid[:, first] - jnp.where(square_lane == 0, column, 0.0)
        column = as_column(out[3, 0:1, :])
        resid[:, last] = resid[:, last] - jnp.where(square_lane == LANES - 1, column, 0.0)

    send_depth(0)
    route(0)

    @pl.loop(0, bands, unroll=2)
    def _(b):
        routed = band_at(resid, b)
        drained = band_at(coef_d, b) * power_five_thirds(routed)
        put_band(drained_sum, b, drained)
        h, soaked = infiltrate(
            routed - drained,
            band_at(soak_out, b),
            band_at(conductivity, b),
            band_at(supply, b),
            wet_at(b),
        )
        put_band(ponded, b, h)
        put_band(soak_out, b, soaked)

    save_soak = pltpu.make_async_copy(soak_out, soak_out_hbm, save_sem.at[0])
    save_soak.start()
    send_depth(1)
    route(1)

    pack_row = lax.broadcasted_iota(jnp.int32, (PACK, LANES), 0)
    lines = [
        (pack_row + t * PACK).astype(jnp.float32).astype(jnp.bfloat16)
        for t in range(REACH_BLOCK // PACK)
    ]
    owners = []
    for t in range(blocks // PACK):
        value = jnp.zeros((PACK, LANES), jnp.int32)
        for i in range(PACK):
            value = jnp.where(pack_row == i, order[t * PACK + i], value)
        owners.append(value.astype(jnp.float32).astype(jnp.bfloat16))
    one = jnp.ones((PACK, LANES), jnp.bfloat16)
    zero = jnp.zeros((PACK, LANES), jnp.bfloat16)

    def drain(b, total):
        routed = band_at(resid, b)
        drained = band_at(coef_d, b) * power_five_thirds(routed)
        put_band(depth_out, b, routed - drained)
        value = band_at(drained_sum, b) + drained
        upper = value.astype(jnp.bfloat16).astype(jnp.float32)
        lower = value - upper
        cell = band_at(reach, b)
        block = lax.shift_right_logical(cell, 7).astype(jnp.float32)
        line = lax.bitwise_and(cell, REACH_BLOCK - 1).astype(jnp.float32)
        for i in range(BAND):

            def spread(x, c):
                row = x[i : i + 1, c * LANES : (c + 1) * LANES]
                return jnp.broadcast_to(row, (PACK, LANES)).astype(jnp.bfloat16)

            left, right = [], []
            for c in range(chunks):
                block_c, line_c = spread(block, c), spread(line, c)
                upper_c, lower_c = spread(upper, c), spread(lower, c)
                hits = [block_c == o for o in owners]
                left.append(
                    jnp.concatenate(
                        [jnp.where(hit, upper_c, zero) for hit in hits]
                        + [jnp.where(hit, lower_c, zero) for hit in hits],
                        axis=0,
                    )
                )
                right.append(
                    jnp.concatenate([jnp.where(line_c == o, one, zero) for o in lines], axis=0)
                )
            total = total + lax.dot_general(
                jnp.concatenate(left, axis=1),
                jnp.concatenate(right, axis=1),
                (((1,), (1,)), ((), ())),
                preferred_element_type=jnp.float32,
            )
        return total

    total = lax.fori_loop(
        0, bands, drain, jnp.zeros((2 * blocks, REACH_BLOCK), jnp.float32)
    )
    save_depth = pltpu.make_async_copy(depth_out, depth_out_hbm, save_sem.at[1])
    save_depth.start()
    total = total[:blocks] + total[blocks:]
    for d in range(n_dev):
        totals[d] = total[d * per_dev : (d + 1) * per_dev]

    @pl.loop(1, n_dev)
    def _(offset):
        total_copy(offset).start()

    arrived[0] = totals[me]

    for side in range(8):
        on_side(side, lambda device, side=side: edge_copy(side, device, side).wait_send())
    for step in range(2):
        for side in range(4):
            on_side(
                side,
                lambda device, side=side, step=step: depth_copy(
                    step, side, device, side
                ).wait_send(),
            )

    @pl.loop(1, n_dev)
    def _(offset):
        total_copy(offset).wait_recv()

    inflow_out[...] = jnp.sum(arrived[...], axis=0)
    save_inflow = pltpu.make_async_copy(inflow_out, inflow_out_hbm, save_sem.at[2])
    save_inflow.start()
    save_soak.wait()
    save_depth.wait()
    save_inflow.wait()

    @pl.loop(1, n_dev)
    def _(offset):
        total_copy(offset).wait_send()


def write_out(*refs):
    sources, targets, held, load, save = refs[:3], refs[3:6], refs[6:9], refs[9], refs[10]
    reads = [pltpu.make_async_copy(s, h, load.at[k]) for k, (s, h) in enumerate(zip(sources, held))]
    writes = [pltpu.make_async_copy(h, t, save.at[k]) for k, (h, t) in enumerate(zip(held, targets))]
    for read in reads:
        read.start()
    for read, write in zip(reads, writes):
        read.wait()
        write.start()
    for write in writes:
        write.wait()


def shards(n_lat, n_lon, *operands):
    depth, order = operands[0], operands[9]
    hbm = pl.BlockSpec(memory_space=pltpu.HBM)
    rows, cols = depth.shape
    tile_rows = operands[7].shape[0]
    n_dev = n_lat * n_lon
    per_dev = order.shape[0] // n_dev
    grid = pltpu.VMEM((rows, cols), jnp.float32)
    results = pl.pallas_call(
        functools.partial(kernel, n_lat, n_lon),
        out_shape=(
            jax.ShapeDtypeStruct((rows, cols), jnp.float32),
            jax.ShapeDtypeStruct((rows, cols), jnp.float32),
            jax.ShapeDtypeStruct((per_dev, REACH_BLOCK), jnp.float32),
        ),
        in_specs=[hbm] * 10,
        out_specs=(hbm, hbm, hbm),
        scratch_shapes=[
            (pltpu.SMEM if k in (5, 7, 9) else pltpu.VMEM)(x.shape, x.dtype)
            for k, x in enumerate(operands)
        ]
        + [
            grid,
            grid,
            pltpu.VMEM((per_dev, REACH_BLOCK), jnp.float32),
            pltpu.SemaphoreType.DMA((10,)),
            pltpu.SemaphoreType.DMA((3,)),
            pltpu.VMEM((tile_rows * BAND, cols), jnp.float32),
            grid,
            grid,
            grid,
            grid,
            grid,
            grid,
            grid,
            pltpu.VMEM((4, 4, BAND, LANES), jnp.float32),
            pltpu.VMEM((4, 4, BAND, LANES), jnp.float32),
            pltpu.VMEM((4, BAND, LANES), jnp.float32),
            pltpu.VMEM((2, 4, BAND, LANES), jnp.float32),
            pltpu.VMEM((2, 4, BAND, LANES), jnp.float32),
            pltpu.VMEM((n_dev, per_dev, REACH_BLOCK), jnp.float32),
            pltpu.VMEM((n_dev, per_dev, REACH_BLOCK), jnp.float32),
            pltpu.SemaphoreType.DMA((8,)),
            pltpu.SemaphoreType.DMA((8,)),
            pltpu.SemaphoreType.DMA((2, 4)),
            pltpu.SemaphoreType.DMA((2, 4)),
            pltpu.SemaphoreType.DMA((n_dev,)),
            pltpu.SemaphoreType.DMA((n_dev,)),
        ],
        compiler_params=pltpu.CompilerParams(
            collective_id=0, has_side_effects=True, vmem_limit_bytes=VMEM_LIMIT
        ),
        name="flow",
    )(*operands)
    return pl.pallas_call(
        write_out,
        out_shape=[jax.ShapeDtypeStruct(x.shape, x.dtype) for x in results],
        in_specs=[hbm] * 3,
        out_specs=[hbm] * 3,
        scratch_shapes=[pltpu.VMEM(x.shape, x.dtype) for x in results]
        + [pltpu.SemaphoreType.DMA((3,)), pltpu.SemaphoreType.DMA((3,))],
        compiler_params=pltpu.CompilerParams(vmem_limit_bytes=VMEM_LIMIT),
        name="write",
    )(*results)


def solution(mesh):
    placed = (P("lat", "lon"),) * 9 + (P(),)
    return jax.shard_map(
        functools.partial(shards, mesh.shape["lat"], mesh.shape["lon"]),
        mesh=mesh,
        in_specs=placed,
        out_specs=(P("lat", "lon"), P("lat", "lon"), P(("lat", "lon"), None)),
        check_vma=False,
    )
```

```python
import functools
import math

import jax
import jax.numpy as jnp
from jax import lax
from jax.experimental import pallas as pl
from jax.experimental.pallas import tpu as pltpu
from jax.sharding import PartitionSpec as P

TILE = 64
REACH_BLOCK = 128
LANES = 128
BAND = 8
PACK = 16
PIECES = 4
VMEM_LIMIT = 60 * 1024 * 1024
MESH = pl.DeviceIdType.MESH

time_step = 0.05
suction = 0.3
slope_floor = 0.25
drain_rate = 0.5

FACE_SCALE = time_step * 2.0 * 0.5 ** (5.0 / 3.0)

STEPS = ((-1, 0), (1, 0), (0, -1), (0, 1), (-1, -1), (-1, 1), (1, -1), (1, 1))
OPPOSITE = (1, 0, 3, 2, 7, 6, 5, 4)
ELEV, ROUGH, WET, RATE = range(4)


def power_five_thirds(value):
    return value * jnp.exp2(jnp.log(value * value) * (1.0 / (3.0 * math.log(2.0))))


def face_flux(coef, depth_sum, head_drop):
    return (
        coef
        * power_five_thirds(depth_sum)
        * (head_drop * lax.rsqrt(jnp.abs(head_drop) + slope_floor))
    )


def infiltrate(level, soaked_sum, conductivity, supply, wet):
    available = level + supply
    potential = time_step * conductivity * (1.0 + suction / soaked_sum)
    soaked = wet * jnp.minimum(potential, jnp.maximum(available, 0.0))
    return available - soaked, soaked_sum + soaked


def kernel(
    n_lat,
    n_lon,
    depth_hbm,
    soakage_hbm,
    elevation_hbm,
    roughness_hbm,
    conductivity_hbm,
    runoff_hbm,
    coarse_hbm,
    wet_tiles_hbm,
    reach_hbm,
    order_hbm,
    depth_out_hbm,
    soak_out_hbm,
    inflow_out_hbm,
    depth,
    soakage,
    elevation,
    roughness,
    conductivity,
    runoff,
    coarse,
    wet_tiles,
    reach,
    order,
    depth_out,
    soak_out,
    inflow_out,
    load_sem,
    save_sem,
    wet_rows,
    ponded,
    resid,
    supply,
    coef_e,
    coef_s,
    coef_d,
    drained_sum,
    own_edge,
    near_edge,
    near_corner,
    own_depth,
    near_depth,
    totals,
    arrived,
    edge_send,
    edge_recv,
    depth_send,
    depth_recv,
    total_send,
    total_recv,
):
    rows, cols = depth.shape
    bands = rows // BAND
    chunks = cols // LANES
    blocks = order.shape[0]
    n_dev = n_lat * n_lon
    per_dev = blocks // n_dev
    num_reaches = blocks * REACH_BLOCK
    lat, lon = lax.axis_index("lat"), lax.axis_index("lon")
    me = lat * n_lon + lon

    loads = [
        pltpu.make_async_copy(src, dst, load_sem.at[k])
        for k, (src, dst) in enumerate(
            (
                (wet_tiles_hbm, wet_tiles),
                (runoff_hbm, runoff),
                (elevation_hbm, elevation),
                (roughness_hbm, roughness),
                (reach_hbm, reach),
                (order_hbm, order),
                (coarse_hbm, coarse),
                (depth_hbm, depth),
                (soakage_hbm, soakage),
                (conductivity_hbm, conductivity),
            )
        )
    ]
    for load in loads:
        load.start()
    near_edge[...] = jnp.zeros_like(near_edge)
    near_corner[...] = jnp.zeros_like(near_corner)
    near_depth[...] = jnp.zeros_like(near_depth)

    barrier = pltpu.get_barrier_semaphore()

    def other(offset):
        device = lax.rem(me + offset, n_dev)
        return (lax.div(device, n_lon), lax.rem(device, n_lon))

    @pl.loop(1, n_dev, unroll=True)
    def _(offset):
        pl.semaphore_signal(barrier, inc=1, device_id=other(offset), device_id_type=MESH)

    def on_side(side, action):
        up, right = STEPS[side]
        row, col = lat + up, lon + right
        inside = (row >= 0) & (row < n_lat) & (col >= 0) & (col < n_lon)

        @pl.when(inside)
        def _():
            action((row, col))

    def edge_copy(side, device, slot):
        if side < 4:
            src, dst = own_edge.at[side], near_edge.at[slot]
        else:
            src, dst = own_edge.at[0, RATE], near_corner.at[slot - 4]
        return pltpu.make_async_remote_copy(
            src_ref=src,
            dst_ref=dst,
            send_sem=edge_send.at[side],
            recv_sem=edge_recv.at[slot],
            device_id=device,
            device_id_type=MESH,
        )

    def depth_copy(step, side, device, slot):
        return pltpu.make_async_remote_copy(
            src_ref=own_depth.at[step, side],
            dst_ref=near_depth.at[step, slot],
            send_sem=depth_send.at[step, side],
            recv_sem=depth_recv.at[step, slot],
            device_id=device,
            device_id_type=MESH,
        )

    def total_copy(offset):
        device = lax.rem(me + offset, n_dev)
        return pltpu.make_async_remote_copy(
            src_ref=totals.at[device],
            dst_ref=arrived.at[offset],
            send_sem=total_send.at[offset],
            recv_sem=total_recv.at[offset],
            device_id=(lax.div(device, n_lon), lax.rem(device, n_lon)),
            device_id_type=MESH,
        )

    lane = lax.broadcasted_iota(jnp.int32, (BAND, LANES), 1)
    wide_lane = lax.broadcasted_iota(jnp.int32, (BAND, cols), 1)
    wide_row = lax.broadcasted_iota(jnp.int32, (BAND, cols), 0)
    square_row = lax.broadcasted_iota(jnp.int32, (rows, LANES), 0)
    square_lane = lax.broadcasted_iota(jnp.int32, (rows, LANES), 1)
    diagonal = square_row == square_lane

    def band_at(ref, b):
        return ref[pl.ds(pl.multiple_of(b * BAND, BAND), BAND), :]

    def put_band(ref, b, value):
        ref[pl.ds(pl.multiple_of(b * BAND, BAND), BAND), :] = value

    def wet_at(b):
        return band_at(wet_rows, lax.div(b, TILE // BAND))

    def below(here, after):
        return pltpu.roll(jnp.where(wide_row == 0, after, here), BAND - 1, 0)

    def above(before, here):
        return pltpu.roll(jnp.where(wide_row == BAND - 1, before, here), 1, 0)

    def east(here):
        return pltpu.roll(here, cols - 1, 1)

    def west(here):
        return pltpu.roll(here, 1, 1)

    def as_row(column):
        return jnp.sum(jnp.where(diagonal, column, 0.0), axis=0, keepdims=True)

    def as_column(row):
        return jnp.sum(jnp.where(diagonal, row, 0.0), axis=1, keepdims=True)

    def pack_edges(ref, put):
        for c in range(chunks):
            cut = slice(c * LANES, (c + 1) * LANES)
            put(0, c, ref[0:1, cut])
            put(1, c, ref[rows - 1 : rows, cut])
        put(2, 0, as_row(ref[:, 0:LANES][:, 0:1]))
        put(3, 0, as_row(ref[:, cols - LANES : cols][:, LANES - 1 : LANES]))

    for load in loads[:4]:
        load.wait()

    tile_rows, tile_cols = wet_tiles.shape
    for tr in range(tile_rows):
        value = jnp.zeros((BAND, cols), jnp.float32)
        for tc in range(tile_cols):
            inside = (wide_lane >= tc * TILE) & (wide_lane < (tc + 1) * TILE)
            value = jnp.where(inside, wet_tiles[tr, tc].astype(jnp.float32), value)
        wet_rows[tr * BAND : (tr + 1) * BAND, :] = value

    own_edge[...] = jnp.zeros_like(own_edge)
    own_depth[...] = jnp.zeros_like(own_depth)

    def put_field(field):
        def put(side, line, value):
            own_edge[side, field, line : line + 1, :] = value

        return put

    pack_edges(elevation, put_field(ELEV))
    pack_edges(roughness, put_field(ROUGH))
    last_tile = (tile_rows - 1) * BAND
    for c in range(chunks):
        cut = slice(c * LANES, (c + 1) * LANES)
        own_edge[0, WET, c : c + 1, :] = wet_rows[0:1, cut]
        own_edge[1, WET, c : c + 1, :] = wet_rows[last_tile : last_tile + 1, cut]
    row_lane = lax.broadcasted_iota(jnp.int32, (1, LANES), 1)
    for side, tc in ((2, 0), (3, tile_cols - 1)):
        value = jnp.zeros((1, LANES), jnp.float32)
        for tr in range(tile_rows):
            inside = (row_lane >= tr * TILE) & (row_lane < (tr + 1) * TILE)
            value = jnp.where(inside, wet_tiles[tr, tc].astype(jnp.float32), value)
        own_edge[side, WET, 0:1, :] = value
    block_cols = runoff.shape[1]
    rates = jnp.zeros((BAND, LANES), jnp.float32)
    for c in range(block_cols):
        rates = jnp.where(lane == c, runoff[0, c], rates)
    for side in range(4):
        own_edge[side, RATE] = rates

    pl.semaphore_wait(barrier, n_dev - 1)
    for side in range(8):
        on_side(side, lambda device, side=side: edge_copy(side, device, OPPOSITE[side]).start())

    for load in loads[4:]:
        load.wait()

    @pl.loop(0, bands, unroll=2)
    def _(b):
        after = jnp.minimum(b + 1, bands - 1)
        rough, wet = band_at(roughness, b), wet_at(b)
        rough_s = below(rough, band_at(roughness, after))
        wet_s = below(wet, wet_at(after))
        value = FACE_SCALE * wet * wet_s / (rough + rough_s)
        put_band(coef_s, b, jnp.where(wide_row + b * BAND == rows - 1, 0.0, value))
        value = FACE_SCALE * wet * east(wet) / (rough + east(rough))
        put_band(coef_e, b, jnp.where(wide_lane == cols - 1, 0.0, value))
        channel = jnp.where(band_at(reach, b) < num_reaches, wet, 0.0)
        put_band(coef_d, b, channel * (time_step * drain_rate) / rough)

    for side in range(8):
        on_side(side, lambda device, side=side: edge_copy(side, device, side).wait_recv())

    def entry(ref_tile, c):
        return jnp.broadcast_to(ref_tile[0:1, c : c + 1], (BAND, cols))

    def rate_row(left, middle, right):
        return (
            [entry(left, block_cols - 1)]
            + [entry(middle, c) for c in range(block_cols)]
            + [entry(right, 0)]
        )

    table = (
        rate_row(near_corner[0], near_edge[0, RATE], near_corner[1])
        + rate_row(near_edge[2, RATE], rates, near_edge[3, RATE])
        + rate_row(near_corner[2], near_edge[1, RATE], near_corner[3])
    )

    @pl.loop(0, bands, unroll=2)
    def _(b):
        index = band_at(coarse, b)
        wet = wet_at(b)
        rate = table[0]
        for k in range(1, len(table)):
            rate = jnp.where(index == k, table[k], rate)
        water = wet * time_step * rate
        put_band(supply, b, water)
        h, soaked = infiltrate(
            band_at(depth, b), band_at(soakage, b), band_at(conductivity, b), water, wet
        )
        put_band(ponded, b, h)
        put_band(soak_out, b, soaked)

    edge_rough = jnp.maximum(own_edge[:, ROUGH] + near_edge[:, ROUGH], 1.0)
    edge_coef = FACE_SCALE * own_edge[:, WET] * near_edge[:, WET] / edge_rough
    edge_drop = own_edge[:, ELEV] - near_edge[:, ELEV]

    def send_depth(step):
        def put(side, line, value):
            own_depth[step, side, line : line + 1, :] = value

        pack_edges(ponded, put)
        for side in range(4):
            on_side(
                side,
                lambda device, side=side: depth_copy(step, side, device, OPPOSITE[side]).start(),
            )

    def route(step):
        def body(b, flux_n):
            after = jnp.minimum(b + 1, bands - 1)
            h, h_after = band_at(ponded, b), band_at(ponded, after)
            head = band_at(elevation, b) + h
            head_after = band_at(elevation, after) + h_after
            flux_s = face_flux(
                band_at(coef_s, b), h + below(h, h_after), head - below(head, head_after)
            )
            flux_e = face_flux(band_at(coef_e, b), h + east(h), head - east(head))
            out = flux_e - west(flux_e) + flux_s - above(flux_n, flux_s)
            put_band(resid, b, h - out)
            return flux_s

        lax.fori_loop(0, bands, body, jnp.zeros((BAND, cols), jnp.float32), unroll=2)
        for side in range(4):
            on_side(
                side, lambda device, side=side: depth_copy(step, side, device, side).wait_recv()
            )
        mine, theirs = own_depth[step], near_depth[step]
        out = face_flux(edge_coef, mine + theirs, edge_drop + (mine - theirs))
        for c in range(chunks):
            cut = slice(c * LANES, (c + 1) * LANES)
            resid[0:1, cut] = resid[0:1, cut] - out[0, c : c + 1, :]
            resid[rows - 1 : rows, cut] = resid[rows - 1 : rows, cut] - out[1, c : c + 1, :]
        first, last = slice(0, LANES), slice(cols - LANES, cols)
        column = as_column(out[2, 0:1, :])
        resid[:, first] = resid[:, first] - jnp.where(square_lane == 0, column, 0.0)
        column = as_column(out[3, 0:1, :])
        resid[:, last] = resid[:, last] - jnp.where(square_lane == LANES - 1, column, 0.0)

    send_depth(0)
    route(0)

    @pl.loop(0, bands, unroll=2)
    def _(b):
        routed = band_at(resid, b)
        drained = band_at(coef_d, b) * power_five_thirds(routed)
        put_band(drained_sum, b, drained)
        h, soaked = infiltrate(
            routed - drained,
            band_at(soak_out, b),
            band_at(conductivity, b),
            band_at(supply, b),
            wet_at(b),
        )
        put_band(ponded, b, h)
        put_band(soak_out, b, soaked)

    save_soak = pltpu.make_async_copy(soak_out, soak_out_hbm, save_sem.at[0])
    save_soak.start()
    send_depth(1)
    route(1)

    pack_row = lax.broadcasted_iota(jnp.int32, (PACK, LANES), 0)
    lines = [
        (pack_row + t * PACK).astype(jnp.float32).astype(jnp.bfloat16)
        for t in range(REACH_BLOCK // PACK)
    ]
    owners = []
    for t in range(blocks // PACK):
        value = jnp.zeros((PACK, LANES), jnp.int32)
        for i in range(PACK):
            value = jnp.where(pack_row == i, order[t * PACK + i], value)
        owners.append(value.astype(jnp.float32).astype(jnp.bfloat16))
    one = jnp.ones((PACK, LANES), jnp.bfloat16)
    zero = jnp.zeros((PACK, LANES), jnp.bfloat16)

    def drain(b, total):
        routed = band_at(resid, b)
        drained = band_at(coef_d, b) * power_five_thirds(routed)
        put_band(depth_out, b, routed - drained)
        value = band_at(drained_sum, b) + drained
        upper = value.astype(jnp.bfloat16).astype(jnp.float32)
        lower = value - upper
        cell = band_at(reach, b)
        block = lax.shift_right_logical(cell, 7).astype(jnp.float32)
        line = lax.bitwise_and(cell, REACH_BLOCK - 1).astype(jnp.float32)
        for i in range(BAND):

            def spread(x, c):
                row = x[i : i + 1, c * LANES : (c + 1) * LANES]
                return jnp.broadcast_to(row, (PACK, LANES)).astype(jnp.bfloat16)

            left, right = [], []
            for c in range(chunks):
                block_c, line_c = spread(block, c), spread(line, c)
                upper_c, lower_c = spread(upper, c), spread(lower, c)
                hits = [block_c == o for o in owners]
                left.append(
                    jnp.concatenate(
                        [jnp.where(hit, upper_c, zero) for hit in hits]
                        + [jnp.where(hit, lower_c, zero) for hit in hits],
                        axis=0,
                    )
                )
                right.append(
                    jnp.concatenate([jnp.where(line_c == o, one, zero) for o in lines], axis=0)
                )
            total = total + lax.dot_general(
                jnp.concatenate(left, axis=1),
                jnp.concatenate(right, axis=1),
                (((1,), (1,)), ((), ())),
                preferred_element_type=jnp.float32,
            )
        return total

    total = lax.fori_loop(
        0, bands, drain, jnp.zeros((2 * blocks, REACH_BLOCK), jnp.float32)
    )
    save_depth = pltpu.make_async_copy(depth_out, depth_out_hbm, save_sem.at[1])
    save_depth.start()
    total = total[:blocks] + total[blocks:]
    for d in range(n_dev):
        totals[d] = total[d * per_dev : (d + 1) * per_dev]

    @pl.loop(1, n_dev, unroll=True)
    def _(offset):
        total_copy(offset).start()

    arrived[0] = totals[me]

    for side in range(8):
        on_side(side, lambda device, side=side: edge_copy(side, device, side).wait_send())
    for step in range(2):
        for side in range(4):
            on_side(
                side,
                lambda device, side=side, step=step: depth_copy(
                    step, side, device, side
                ).wait_send(),
            )

    @pl.loop(1, n_dev, unroll=True)
    def _(offset):
        total_copy(offset).wait_recv()

    inflow_out[...] = jnp.sum(arrived[...], axis=0)
    save_inflow = pltpu.make_async_copy(inflow_out, inflow_out_hbm, save_sem.at[2])
    save_inflow.start()
    save_soak.wait()
    save_depth.wait()
    save_inflow.wait()

    @pl.loop(1, n_dev, unroll=True)
    def _(offset):
        total_copy(offset).wait_send()


def pieces(results):
    cuts = []
    for k, x in enumerate(results):
        count = PIECES if x.shape[0] % (PIECES * BAND) == 0 else 1
        size = x.shape[0] // count
        cuts += [(k, pl.ds(p * size, size)) for p in range(count)]
    return cuts


def write_out(*refs):
    sources, targets, held, load, save = refs[:3], refs[3:6], refs[6:9], refs[9], refs[10]
    reads, writes = [], []
    for n, (k, cut) in enumerate(pieces(sources)):
        here = held[k].at[cut]
        reads.append(pltpu.make_async_copy(sources[k].at[cut], here, load.at[n]))
        writes.append(pltpu.make_async_copy(here, targets[k].at[cut], save.at[n]))
    for read in reads:
        read.start()
    for read, write in zip(reads, writes):
        read.wait()
        write.start()
    for write in writes:
        write.wait()


def shards(n_lat, n_lon, *operands):
    depth, order = operands[0], operands[9]
    hbm = pl.BlockSpec(memory_space=pltpu.HBM)
    rows, cols = depth.shape
    tile_rows = operands[7].shape[0]
    n_dev = n_lat * n_lon
    per_dev = order.shape[0] // n_dev
    grid = pltpu.VMEM((rows, cols), jnp.float32)
    results = pl.pallas_call(
        functools.partial(kernel, n_lat, n_lon),
        out_shape=(
            jax.ShapeDtypeStruct((rows, cols), jnp.float32),
            jax.ShapeDtypeStruct((rows, cols), jnp.float32),
            jax.ShapeDtypeStruct((per_dev, REACH_BLOCK), jnp.float32),
        ),
        in_specs=[hbm] * 10,
        out_specs=(hbm, hbm, hbm),
        scratch_shapes=[
            (pltpu.SMEM if k in (5, 7, 9) else pltpu.VMEM)(x.shape, x.dtype)
            for k, x in enumerate(operands)
        ]
        + [
            grid,
            grid,
            pltpu.VMEM((per_dev, REACH_BLOCK), jnp.float32),
            pltpu.SemaphoreType.DMA((10,)),
            pltpu.SemaphoreType.DMA((3,)),
            pltpu.VMEM((tile_rows * BAND, cols), jnp.float32),
            grid,
            grid,
            grid,
            grid,
            grid,
            grid,
            grid,
            pltpu.VMEM((4, 4, BAND, LANES), jnp.float32),
            pltpu.VMEM((4, 4, BAND, LANES), jnp.float32),
            pltpu.VMEM((4, BAND, LANES), jnp.float32),
            pltpu.VMEM((2, 4, BAND, LANES), jnp.float32),
            pltpu.VMEM((2, 4, BAND, LANES), jnp.float32),
            pltpu.VMEM((n_dev, per_dev, REACH_BLOCK), jnp.float32),
            pltpu.VMEM((n_dev, per_dev, REACH_BLOCK), jnp.float32),
            pltpu.SemaphoreType.DMA((8,)),
            pltpu.SemaphoreType.DMA((8,)),
            pltpu.SemaphoreType.DMA((2, 4)),
            pltpu.SemaphoreType.DMA((2, 4)),
            pltpu.SemaphoreType.DMA((n_dev,)),
            pltpu.SemaphoreType.DMA((n_dev,)),
        ],
        compiler_params=pltpu.CompilerParams(
            collective_id=0, has_side_effects=True, vmem_limit_bytes=VMEM_LIMIT
        ),
        name="flow",
    )(*operands)
    return pl.pallas_call(
        write_out,
        out_shape=[jax.ShapeDtypeStruct(x.shape, x.dtype) for x in results],
        in_specs=[hbm] * 3,
        out_specs=[hbm] * 3,
        scratch_shapes=[pltpu.VMEM(x.shape, x.dtype) for x in results]
        + [pltpu.SemaphoreType.DMA((len(pieces(results)),))] * 2,
        compiler_params=pltpu.CompilerParams(vmem_limit_bytes=VMEM_LIMIT),
        name="write",
    )(*results)


def solution(mesh):
    placed = (P("lat", "lon"),) * 9 + (P(),)
    return jax.shard_map(
        functools.partial(shards, mesh.shape["lat"], mesh.shape["lon"]),
        mesh=mesh,
        in_specs=placed,
        out_specs=(P("lat", "lon"), P("lat", "lon"), P(("lat", "lon"), None)),
        check_vma=False,
    )
```
